32 devices in a mesh: grp: 2 (over y), cpl: 4 (over z), mem: 4 (over x, core).
Axes of the slice: x: 2, y: 2, z: 4, core: 2. Of those that a mesh axis runs over, the one named last changes fastest.
Arguments:
- sources: bfloat16 [16, 128, 4, 720], P(('grp', 'cpl'), None, 'mem'), parts along dimension 0, may hold values from -6 to 6
- weights: bfloat16 [64, 8, 128, 128], P(('grp', 'cpl')), parts along dimension 0, may hold values from -0.375 to 0.375
- cover_source: int32 [64, 8], P(('grp', 'cpl')), parts along dimension 0, may hold values from 0 to 3, as said below
- cover_count: int32 [64], P(('grp', 'cpl')), parts along dimension 0, may hold values from 4 to 8
- send_pick: int32 [8, 4], P('grp'), parts along dimension 0, may hold values from 0 to 1
Outputs:
- remapped: bfloat16 [64, 128, 4, 720], P(('grp', 'cpl'), None, 'mem'), parts along dimension 0
- ens_mean: float32 [64, 128, 720], P(('grp', 'cpl'), 'mem'), parts along dimension 0
The draws below stay inside these ranges and needn't reach their ends.
There are 2 independent parts, one for each index of `grp`. The reference program is written for one: setup_inputs(seed, part) draws one part's arguments, and reference() takes and returns one part's arrays. A program takes and returns all parts, laid end to end along the dimension named above; each array names one. Nothing has to cross between parts.
Inputs may be any that keep to these rules, and one draw needn't show every extreme that they name: `cover_source`: among the slots k < 4 of the targets of one coupler device, every component device is named at least once.
All inputs are finite; a program needn't handle non-finite values.
Results may differ from the reference program's by a relative error of at most 0.001.
Values may be sent and summed in bfloat16 or wider, within the bound.
A program may use at most 64 MiB of HBM per device.

```python
import jax
import jax.numpy as jnp
from jax import lax

NODES = 128
K = 8
SB = 2
TB = 8
FL = 720
MEMBERS = 4
BLOCKS = 8
TARGETS = 32
N_CPL = 4


def draw_cover_source(key, part):
    key = jax.random.fold_in(key, 7)
    device_keys = jax.random.split(jax.random.fold_in(key, 1), N_CPL)
    orders = jax.vmap(lambda one_key: jax.random.permutation(one_key, N_CPL))(device_keys)
    others = jax.random.randint(jax.random.fold_in(key, 2), (N_CPL, TB, K), 0, N_CPL)
    slot_number = jnp.arange(K, dtype=jnp.int32)[None, :] * TB + jnp.arange(TB, dtype=jnp.int32)[:, None]
    covered = jnp.take(orders, slot_number % N_CPL, axis=1)
    first_half = jnp.arange(K, dtype=jnp.int32)[None, None, :] < K // 2
    chosen = jnp.where(first_half, covered, others)
    return chosen.reshape(TARGETS, K).astype(jnp.int32)


def plant(array, own_key, smallest, largest):
    index_at = [jax.random.randint(jax.random.fold_in(own_key, axis), (), 0, length) for axis, length in enumerate(array.shape)]
    longest = array.shape.index(max(array.shape))
    next_to = index_at[:longest] + [(index_at[longest] + 1) % array.shape[longest]] + index_at[longest + 1:]
    return array.at[tuple(index_at)].set(smallest).at[tuple(next_to)].set(largest)


def levels(key, dims, pieces, least, high):
    def one(position, parts):
        heights = jax.random.uniform(jax.random.fold_in(jax.random.fold_in(key, 6), position), (parts,), jnp.float32, least / len(pieces), high / len(pieces))
        return jnp.repeat(jnp.exp(heights), dims[position] // parts).reshape((-1,) + (1,) * (len(dims) - position - 1))

    loudness = one(*pieces[0])
    for cut in pieces[1:]:
        loudness = loudness * one(*cut)
    return loudness


def gaussian(key, dims, spread, reach, shards=(), kind=jnp.bfloat16):
    result = jax.random.normal(key, dims, jnp.float32) * spread
    if len(shards) > 0:
        result = levels(key, dims, shards, -0.22, 0.18) * result
    return jnp.clip(result, min=-reach, max=reach).astype(kind)


def setup_inputs(seed: int = 0, part: int = 0) -> dict:
    key_list = jax.random.split(jax.random.key(seed), 6)
    part_splits = jax.random.split(jax.random.fold_in(key_list[5], part), 6)
    return {
        "sources": gaussian(part_splits[0], (BLOCKS, NODES, MEMBERS, FL), 1.0, 6.0, ((0, 4), (2, 4))),
        "weights": gaussian(part_splits[1], (TARGETS, K, NODES, NODES), (2 * NODES) ** -0.5, 0.375, ((0, 4),)),
        "cover_source": draw_cover_source(jax.random.fold_in(jax.random.fold_in(key_list[5], part), 71), part),
        "cover_count": plant(jax.random.randint(part_splits[3], (TARGETS,), K // 2, K + 1), jax.random.fold_in(part_splits[3], 1), K // 2, K).astype(jnp.int32),
        "send_pick": plant(jax.random.randint(part_splits[4], (N_CPL, N_CPL), 0, SB), jax.random.fold_in(part_splits[4], 1), 0, SB - 1).astype(jnp.int32),
    }


def limit(high_sum, lower_bound, upper_bound):
    center = jnp.mean(high_sum, axis=1)
    top_value = jnp.max(high_sum, axis=1)
    bottom_value = jnp.min(high_sum, axis=1)
    rising = (upper_bound - center) / (top_value - center + 0.25)
    falling = (center - lower_bound) / (center - bottom_value + 0.25)
    factor = jnp.clip(jnp.minimum(rising, falling), 0.0, 1.0)
    return center[:, None] + factor[:, None] * (high_sum - center[:, None])


def reference(sources, weights, cover_source, cover_count, send_pick):
    owner = jnp.arange(TARGETS, dtype=jnp.int32) // TB
    picked = send_pick[cover_source, owner[:, None]]
    block_index = (cover_source * SB + picked).astype(jnp.int32)
    live_mask = jnp.arange(K, dtype=jnp.int32)[None, :] < cover_count[:, None]

    def per_target(items):
        weight_set, index_set, mask_set = items
        blocks = jnp.take(sources, index_set, axis=0)
        masked = jnp.where(mask_set[:, None, None], weight_set, jnp.zeros((), weight_set.dtype))
        left_side = jnp.transpose(masked, (1, 0, 2)).reshape(NODES, K * NODES).astype(jnp.float32)
        right_side = blocks.reshape(K * NODES, MEMBERS * FL).astype(jnp.float32)
        high_sum = jnp.dot(left_side, right_side, precision=lax.Precision.HIGHEST).reshape(1, NODES, MEMBERS, FL)
        lowest = jnp.where(mask_set[:, None, None], jnp.min(blocks, axis=1).astype(jnp.float32), jnp.inf)
        highest = jnp.where(mask_set[:, None, None], jnp.max(blocks, axis=1).astype(jnp.float32), -jnp.inf)
        lower_bound = jnp.min(lowest, axis=0)[None]
        upper_bound = jnp.max(highest, axis=0)[None]
        return limit(high_sum, lower_bound, upper_bound)[0]

    limited = lax.map(per_target, (weights, block_index, live_mask))
    return limited.astype(jnp.bfloat16), jnp.sum(limited, axis=2) / MEMBERS
```

```python
import functools

import jax
import jax.numpy as jnp
from jax import lax
from jax.experimental import pallas as pl
from jax.experimental.pallas import tpu as pltpu
from jax.sharding import PartitionSpec as P

MESH = pl.DeviceIdType.MESH
WIDTH = 128
GROUP = 4


def kernel(
    n_cpl,
    n_mem,
    cover_source,
    cover_count,
    send_pick,
    sources,
    weights,
    remapped,
    ens_mean,
    outgoing,
    pool,
    flipped,
    low,
    high,
    held,
    *rest,
):
    stages = n_mem.bit_length() - 1
    totals = rest[:stages]
    landed = rest[stages : 2 * stages]
    pool_send, pool_recv, weight_sem = rest[2 * stages : 2 * stages + 3]
    stage_send = rest[2 * stages + 3 : 3 * stages + 3]
    stage_recv = rest[3 * stages + 3 : 4 * stages + 3]
    targets, slots, nodes, _ = weights.shape
    levels = sources.shape[1]
    pieces = pl.cdiv(levels, WIDTH)
    groups = targets // GROUP
    share = nodes // n_mem
    me = lax.axis_index("cpl")
    member = lax.axis_index("mem")
    bits = [lax.rem(lax.div(member, 1 << s), 2) for s in range(stages)]
    partners = [member + (1 - 2 * bits[s]) * (1 << s) for s in range(stages)]

    weight_copy = pltpu.make_async_copy(weights, held, weight_sem)
    weight_copy.start()

    barrier = pltpu.get_barrier_semaphore()

    @pl.loop(1, n_cpl)
    def _(distance):
        pl.semaphore_signal(
            barrier, inc=1, device_id={"cpl": lax.rem(me + distance, n_cpl)}, device_id_type=MESH
        )

    for s in range(stages):
        pl.semaphore_signal(barrier, inc=1, device_id={"mem": partners[s]}, device_id_type=MESH)

    def rows_of(piece):
        return piece * WIDTH, min(WIDTH, levels - piece * WIDTH)

    def pool_copy(piece, distance, slot):
        start, size = rows_of(piece)
        return pltpu.make_async_remote_copy(
            src_ref=outgoing.at[distance - 1, pl.ds(start, size)],
            dst_ref=pool.at[slot, pl.ds(start, size)],
            send_sem=pool_send.at[piece, distance - 1],
            recv_sem=pool_recv.at[piece, distance - 1],
            device_id={"cpl": lax.rem(me + distance, n_cpl)},
            device_id_type=MESH,
        )

    def fill(piece):
        start, size = rows_of(piece)

        @pl.loop(1, n_cpl)
        def _(distance):
            chosen = send_pick[me, lax.rem(me + distance, n_cpl)]
            outgoing[distance - 1, pl.ds(start, size)] = sources[chosen, pl.ds(start, size)]

    def send(piece):
        @pl.loop(1, n_cpl)
        def _(distance):
            pool_copy(piece, distance, me).start()

    fill(0)
    pl.semaphore_wait(barrier, n_cpl - 1 + stages)
    send(0)
    for piece in range(1, pieces):
        fill(piece)
        send(piece)

    own = send_pick[me, me]
    pool[me, pl.ds(0, levels)] = sources[own]
    if pieces * WIDTH > levels:
        tail = pieces * WIDTH - levels
        pool[:, pl.ds(levels, tail)] = jnp.zeros((n_cpl, tail, nodes), pool.dtype)
    flipped[n_cpl] = jnp.zeros(flipped.shape[1:], flipped.dtype)
    weight_copy.wait()

    def stage_copy(s, piece, group):
        spot = (piece, group) if s == 0 else (piece,)
        return pltpu.make_async_remote_copy(
            src_ref=totals[s].at[spot + (1 - bits[s],)],
            dst_ref=landed[s].at[spot],
            send_sem=stage_send[s].at[spot],
            recv_sem=stage_recv[s].at[spot],
            device_id={"mem": partners[s]},
            device_id_type=MESH,
        )

    def remap(piece, target):
        start, size = rows_of(piece)
        count = cover_count[target]
        first = cover_source[target, 0]
        terms, lowest, highest = [], [], []
        for k in range(slots):
            block = cover_source[target, k]
            live = k < count
            terms.append(flipped[jnp.where(live, block, n_cpl)])
            ranged = jnp.where(live, block, first)
            lowest.append(low[ranged])
            highest.append(high[ranged])
        left = jnp.concatenate([held[target, k] for k in range(slots)], axis=1)
        right = jnp.concatenate(terms, axis=0)
        summed = jnp.dot(left, right, preferred_element_type=jnp.float32)
        lower = functools.reduce(jnp.minimum, lowest)
        upper = functools.reduce(jnp.maximum, highest)
        center = jnp.sum(summed, axis=0, keepdims=True) * (1.0 / nodes)
        top = jnp.max(summed, axis=0, keepdims=True)
        bottom = jnp.min(summed, axis=0, keepdims=True)
        rising = (upper - center) / (top - center + 0.25)
        falling = (center - lower) / (center - bottom + 0.25)
        factor = jnp.clip(jnp.minimum(rising, falling), 0.0, 1.0)
        limited = center + factor * (summed - center)
        turned = limited.astype(jnp.bfloat16).T
        remapped[target, pl.ds(start, size)] = turned[:size]
        return limited

    def collect(piece):
        last = stages - 1
        start, size = rows_of(piece)
        stage_copy(last, piece, 0).wait_recv()
        total = totals[last][piece, bits[last], 0] + landed[last][piece, 0]
        ens_mean[:, :, pl.ds(start, size)] = (total * (1.0 / n_mem))[:, :, :size]

    for piece in range(pieces):
        start, size = rows_of(piece)

        @pl.loop(1, n_cpl)
        def _(distance):
            pool_copy(piece, distance, lax.rem(me - distance + n_cpl, n_cpl)).wait_recv()

        @pl.loop(0, n_cpl)
        def _(block):
            values = pool[block, pl.ds(piece * WIDTH, WIDTH)].T
            flipped[block] = values
            wide = values.astype(jnp.float32)
            low[block] = jnp.min(wide, axis=0, keepdims=True)
            high[block] = jnp.max(wide, axis=0, keepdims=True)

        @pl.loop(0, groups)
        def _(group):
            for one in range(GROUP):
                limited = remap(piece, group * GROUP + one)
                for q in range(n_mem):
                    totals[0][piece, group, q % 2, q // 2, one] = limited[q * share : (q + 1) * share]
            stage_copy(0, piece, group).start()

        for s in range(1, stages):
            parts = n_mem >> s
            if s == 1:
                for group in range(groups):
                    stage_copy(0, piece, group).wait_recv()
                    for q in range(parts):
                        totals[1][piece, q % 2, q // 2, pl.ds(group * GROUP, GROUP)] = (
                            totals[0][piece, group, bits[0], q] + landed[0][piece, group, q]
                        )
            else:
                stage_copy(s - 1, piece, 0).wait_recv()
                for q in range(parts):
                    totals[s][piece, q % 2, q // 2] = (
                        totals[s - 1][piece, bits[s - 1], q] + landed[s - 1][piece, q]
                    )
            stage_copy(s, piece, 0).start()
        if piece > 0:
            collect(piece - 1)
    collect(pieces - 1)

    for piece in range(pieces):

        @pl.loop(1, n_cpl)
        def _(distance):
            pool_copy(piece, distance, me).wait_send()

        for group in range(groups):
            stage_copy(0, piece, group).wait_send()
        for s in range(1, stages):
            stage_copy(s, piece, 0).wait_send()


def local(n_cpl, n_mem, sources, weights, cover_source, cover_count, send_pick):
    blocks, nodes, members, levels = sources.shape
    targets, slots = cover_source.shape
    pieces = pl.cdiv(levels, WIDTH)
    padded = pieces * WIDTH
    groups = targets // GROUP
    share = nodes // n_mem
    stages = n_mem.bit_length() - 1
    turned = jnp.transpose(sources, (0, 2, 3, 1)).reshape(blocks, levels, nodes)
    totals, landed, sems = [], [], []
    for s in range(stages):
        half = (n_mem >> s) // 2
        if s == 0:
            lead, depth = (pieces, groups), GROUP
        else:
            lead, depth = (pieces,), targets
        totals.append(pltpu.VMEM(lead + (2, half, depth, share, WIDTH), jnp.float32))
        landed.append(pltpu.VMEM(lead + (half, depth, share, WIDTH), jnp.float32))
        sems.append(pltpu.SemaphoreType.DMA(lead))
    vmem = pl.BlockSpec(memory_space=pltpu.VMEM)
    smem = pl.BlockSpec(memory_space=pltpu.SMEM)
    remapped, ens_mean = pl.pallas_call(
        functools.partial(kernel, n_cpl, n_mem),
        out_shape=(
            jax.ShapeDtypeStruct((targets, levels, nodes), jnp.bfloat16),
            jax.ShapeDtypeStruct((targets, share, levels), jnp.float32),
        ),
        in_specs=[smem, smem, smem, vmem, pl.BlockSpec(memory_space=pl.ANY)],
        out_specs=(vmem, vmem),
        scratch_shapes=[
            pltpu.VMEM((n_cpl - 1, levels, nodes), jnp.bfloat16),
            pltpu.VMEM((n_cpl, padded, nodes), jnp.bfloat16),
            pltpu.VMEM((n_cpl + 1, nodes, WIDTH), jnp.bfloat16),
            pltpu.VMEM((n_cpl, 1, WIDTH), jnp.float32),
            pltpu.VMEM((n_cpl, 1, WIDTH), jnp.float32),
            pltpu.VMEM((targets, slots, nodes, nodes), jnp.bfloat16),
            *totals,
            *landed,
            pltpu.SemaphoreType.DMA((pieces, n_cpl - 1)),
            pltpu.SemaphoreType.DMA((pieces, n_cpl - 1)),
            pltpu.SemaphoreType.DMA,
            *sems,
            *sems,
        ],
        compiler_params=pltpu.CompilerParams(
            collective_id=0, has_side_effects=True, vmem_limit_bytes=56 * 1024 * 1024
        ),
        cost_estimate=pl.CostEstimate(
            flops=2 * targets * slots * nodes * nodes * levels,
            bytes_accessed=weights.size * 2 + targets * levels * nodes * 4,
            transcendentals=0,
        ),
    )(cover_source, cover_count, send_pick, turned, weights)
    remapped = jnp.transpose(remapped.reshape(targets, members, levels, nodes), (0, 3, 1, 2))
    return remapped, ens_mean


def solution(mesh):
    placed = (
        P(("grp", "cpl"), None, "mem", None),
        P(("grp", "cpl"), None, None, None),
        P(("grp", "cpl"), None),
        P(("grp", "cpl")),
        P("grp", None),
    )
    return jax.shard_map(
        functools.partial(local, mesh.shape["cpl"], mesh.shape["mem"]),
        mesh=mesh,
        in_specs=placed,
        out_specs=(P(("grp", "cpl"), None, "mem", None), P(("grp", "cpl"), "mem", None)),
        check_vma=False,
    )
```

```python
import functools

import jax
import jax.numpy as jnp
from jax import lax
from jax.experimental import pallas as pl
from jax.experimental.pallas import tpu as pltpu
from jax.sharding import PartitionSpec as P

MESH = pl.DeviceIdType.MESH
WIDTH = 128
AHEAD = 2
GROUP = 4


def kernel(
    n_cpl,
    n_mem,
    cover_source,
    cover_count,
    send_pick,
    sources,
    weights,
    remapped,
    ens_mean,
    outgoing,
    pool,
    flipped,
    low,
    high,
    held,
    limited_out,
    mean_out,
    *rest,
):
    stages = n_mem.bit_length() - 1
    totals = rest[:stages]
    landed = rest[stages : 2 * stages]
    pool_send, pool_recv, weight_sem, limited_sem, mean_sem = rest[2 * stages : 2 * stages + 5]
    stage_send = rest[2 * stages + 5 : 3 * stages + 5]
    stage_recv = rest[3 * stages + 5 : 4 * stages + 5]
    targets, slots, nodes, _ = weights.shape
    levels = sources.shape[1]
    pieces = pl.cdiv(levels, WIDTH)
    groups = targets // GROUP
    share = nodes // n_mem
    me = lax.axis_index("cpl")
    member = lax.axis_index("mem")
    bits = [lax.rem(lax.div(member, 1 << s), 2) for s in range(stages)]
    partners = [member + (1 - 2 * bits[s]) * (1 << s) for s in range(stages)]

    weight_copy = pltpu.make_async_copy(weights, held, weight_sem)
    weight_copy.start()

    barrier = pltpu.get_barrier_semaphore()

    @pl.loop(1, n_cpl)
    def _(distance):
        pl.semaphore_signal(
            barrier, inc=1, device_id={"cpl": lax.rem(me + distance, n_cpl)}, device_id_type=MESH
        )

    for s in range(stages):
        pl.semaphore_signal(barrier, inc=1, device_id={"mem": partners[s]}, device_id_type=MESH)

    def rows_of(piece):
        return piece * WIDTH, min(WIDTH, levels - piece * WIDTH)

    def pool_copy(piece, distance, slot):
        start, size = rows_of(piece)
        return pltpu.make_async_remote_copy(
            src_ref=outgoing.at[distance - 1, pl.ds(start, size)],
            dst_ref=pool.at[slot, pl.ds(start, size)],
            send_sem=pool_send.at[piece, distance - 1],
            recv_sem=pool_recv.at[piece, distance - 1],
            device_id={"cpl": lax.rem(me + distance, n_cpl)},
            device_id_type=MESH,
        )

    def fill(piece):
        start, size = rows_of(piece)

        @pl.loop(1, n_cpl)
        def _(distance):
            chosen = send_pick[me, lax.rem(me + distance, n_cpl)]
            outgoing[distance - 1, pl.ds(start, size)] = sources[chosen, pl.ds(start, size)]

    def send(piece):
        @pl.loop(1, n_cpl)
        def _(distance):
            pool_copy(piece, distance, me).start()

    fill(0)
    pl.semaphore_wait(barrier, n_cpl - 1 + stages)
    send(0)
    for piece in range(1, pieces):
        fill(piece)
        if piece < AHEAD:
            send(piece)

    own = send_pick[me, me]
    pool[me, pl.ds(0, levels)] = sources[own]
    if pieces * WIDTH > levels:
        tail = pieces * WIDTH - levels
        pool[:, pl.ds(levels, tail)] = jnp.zeros((n_cpl, tail, nodes), pool.dtype)
    flipped[n_cpl] = jnp.zeros(flipped.shape[1:], flipped.dtype)
    weight_copy.wait()

    def stage_copy(s, piece, group):
        spot = (piece, group)
        return pltpu.make_async_remote_copy(
            src_ref=totals[s].at[spot + (1 - bits[s],)],
            dst_ref=landed[s].at[spot],
            send_sem=stage_send[s].at[spot],
            recv_sem=stage_recv[s].at[spot],
            device_id={"mem": partners[s]},
            device_id_type=MESH,
        )

    def remap(piece, target):
        start, size = rows_of(piece)
        count = cover_count[target]
        first = cover_source[target, 0]
        terms, lowest, highest = [], [], []
        for k in range(slots):
            block = cover_source[target, k]
            live = k < count
            terms.append(flipped[jnp.where(live, block, n_cpl)])
            ranged = jnp.where(live, block, first)
            lowest.append(low[ranged])
            highest.append(high[ranged])
        left = jnp.concatenate([held[target, k] for k in range(slots)], axis=1)
        right = jnp.concatenate(terms, axis=0)
        summed = jnp.dot(left, right, preferred_element_type=jnp.float32)
        lower = functools.reduce(jnp.minimum, lowest)
        upper = functools.reduce(jnp.maximum, highest)
        center = jnp.sum(summed, axis=0, keepdims=True) * (1.0 / nodes)
        top = jnp.max(summed, axis=0, keepdims=True)
        bottom = jnp.min(summed, axis=0, keepdims=True)
        rising = (upper - center) / (top - center + 0.25)
        falling = (center - lower) / (center - bottom + 0.25)
        factor = jnp.clip(jnp.minimum(rising, falling), 0.0, 1.0)
        limited = center + factor * (summed - center)
        turned = limited.astype(jnp.bfloat16).T
        limited_out[target, pl.ds(start, size)] = turned[:size]
        return limited

    def limited_copy(piece):
        start, size = rows_of(piece)
        return pltpu.make_async_copy(
            limited_out.at[:, pl.ds(start, size)],
            remapped.at[:, pl.ds(start, size)],
            limited_sem.at[piece],
        )

    def mean_copy(piece):
        start, size = rows_of(piece)
        return pltpu.make_async_copy(
            mean_out.at[:, :, pl.ds(start, size)],
            ens_mean.at[:, :, pl.ds(start, size)],
            mean_sem.at[piece],
        )

    def collect(piece):
        last = stages - 1
        start, size = rows_of(piece)
        for group in range(groups):
            stage_copy(last, piece, group).wait_recv()
            total = totals[last][piece, group, bits[last], 0] + landed[last][piece, group, 0]
            mean_out[pl.ds(group * GROUP, GROUP), :, pl.ds(start, size)] = (
                total * (1.0 / n_mem)
            )[:, :, :size]
        mean_copy(piece).start()

    for piece in range(pieces):
        start, size = rows_of(piece)

        @pl.loop(1, n_cpl)
        def _(distance):
            pool_copy(piece, distance, lax.rem(me - distance + n_cpl, n_cpl)).wait_recv()

        if piece + AHEAD < pieces:
            send(piece + AHEAD)

        @pl.loop(0, n_cpl)
        def _(block):
            values = pool[block, pl.ds(piece * WIDTH, WIDTH)].T
            flipped[block] = values
            wide = values.astype(jnp.float32)
            low[block] = jnp.min(wide, axis=0, keepdims=True)
            high[block] = jnp.max(wide, axis=0, keepdims=True)

        @pl.loop(0, groups)
        def _(group):
            for one in range(GROUP):
                limited = remap(piece, group * GROUP + one)
                for q in range(n_mem):
                    totals[0][piece, group, q % 2, q // 2, one] = limited[q * share : (q + 1) * share]
            stage_copy(0, piece, group).start()

        limited_copy(piece).start()
        for s in range(1, stages):
            for group in range(groups):
                stage_copy(s - 1, piece, group).wait_recv()
                for q in range(n_mem >> s):
                    totals[s][piece, group, q % 2, q // 2] = (
                        totals[s - 1][piece, group, bits[s - 1], q] + landed[s - 1][piece, group, q]
                    )
                stage_copy(s, piece, group).start()
        if piece > 0:
            collect(piece - 1)
    collect(pieces - 1)

    for piece in range(pieces):

        @pl.loop(1, n_cpl)
        def _(distance):
            pool_copy(piece, distance, me).wait_send()

        for group in range(groups):
            for s in range(stages):
                stage_copy(s, piece, group).wait_send()
        limited_copy(piece).wait()
        mean_copy(piece).wait()


def local(n_cpl, n_mem, sources, weights, cover_source, cover_count, send_pick):
    blocks, nodes, members, levels = sources.shape
    targets, slots = cover_source.shape
    pieces = pl.cdiv(levels, WIDTH)
    padded = pieces * WIDTH
    groups = targets // GROUP
    share = nodes // n_mem
    stages = n_mem.bit_length() - 1
    turned = jnp.transpose(sources, (0, 2, 3, 1)).reshape(blocks, levels, nodes)
    totals, landed, sems = [], [], []
    for s in range(stages):
        half = (n_mem >> s) // 2
        lead = (pieces, groups)
        totals.append(pltpu.VMEM(lead + (2, half, GROUP, share, WIDTH), jnp.float32))
        landed.append(pltpu.VMEM(lead + (half, GROUP, share, WIDTH), jnp.float32))
        sems.append(pltpu.SemaphoreType.DMA(lead))
    vmem = pl.BlockSpec(memory_space=pltpu.VMEM)
    whole = pl.BlockSpec(memory_space=pl.ANY)
    smem = pl.BlockSpec(memory_space=pltpu.SMEM)
    remapped, ens_mean = pl.pallas_call(
        functools.partial(kernel, n_cpl, n_mem),
        out_shape=(
            jax.ShapeDtypeStruct((targets, levels, nodes), jnp.bfloat16),
            jax.ShapeDtypeStruct((targets, share, levels), jnp.float32),
        ),
        in_specs=[smem, smem, smem, vmem, pl.BlockSpec(memory_space=pltpu.HBM)],
        out_specs=(whole, whole),
        scratch_shapes=[
            pltpu.VMEM((n_cpl - 1, levels, nodes), jnp.bfloat16),
            pltpu.VMEM((n_cpl, padded, nodes), jnp.bfloat16),
            pltpu.VMEM((n_cpl + 1, nodes, WIDTH), jnp.bfloat16),
            pltpu.VMEM((n_cpl, 1, WIDTH), jnp.float32),
            pltpu.VMEM((n_cpl, 1, WIDTH), jnp.float32),
            pltpu.VMEM((targets, slots, nodes, nodes), jnp.bfloat16),
            pltpu.VMEM((targets, levels, nodes), jnp.bfloat16),
            pltpu.VMEM((targets, share, levels), jnp.float32),
            *totals,
            *landed,
            pltpu.SemaphoreType.DMA((pieces, n_cpl - 1)),
            pltpu.SemaphoreType.DMA((pieces, n_cpl - 1)),
            pltpu.SemaphoreType.DMA,
            pltpu.SemaphoreType.DMA((pieces,)),
            pltpu.SemaphoreType.DMA((pieces,)),
            *sems,
            *sems,
        ],
        compiler_params=pltpu.CompilerParams(
            collective_id=0, has_side_effects=True, vmem_limit_bytes=(17 + n_cpl // 2) * 1024 * 1024
        ),
        cost_estimate=pl.CostEstimate(
            flops=2 * targets * slots * nodes * nodes * levels,
            bytes_accessed=weights.size * 2 + targets * levels * nodes * 4,
            transcendentals=0,
        ),
    )(cover_source, cover_count, send_pick, turned, weights)
    remapped = jnp.transpose(remapped.reshape(targets, members, levels, nodes), (0, 3, 1, 2))
    return remapped, ens_mean


def solution(mesh):
    placed = (
        P(("grp", "cpl"), None, "mem", None),
        P(("grp", "cpl"), None, None, None),
        P(("grp", "cpl"), None),
        P(("grp", "cpl")),
        P("grp", None),
    )
    return jax.shard_map(
        functools.partial(local, mesh.shape["cpl"], mesh.shape["mem"]),
        mesh=mesh,
        in_specs=placed,
        out_specs=(P(("grp", "cpl"), None, "mem", None), P(("grp", "cpl"), "mem", None)),
        check_vma=False,
    )
```

```python
import functools

import jax
import jax.numpy as jnp
from jax import lax
from jax.experimental import pallas as pl
from jax.experimental.pallas import tpu as pltpu
from jax.sharding import PartitionSpec as P

MESH = pl.DeviceIdType.MESH
WIDTH = 128
AHEAD = 2
STEPS = 32000.0
GROUP = 4


def kernel(
    n_cpl,
    n_mem,
    cover_source,
    cover_count,
    send_pick,
    sources,
    weights,
    remapped,
    ens_mean,
    outgoing,
    pool,
    flipped,
    low,
    high,
    held,
    limited_out,
    mean_out,
    *rest,
):
    stages = n_mem.bit_length() - 1
    halves, first_landed, *rest = rest
    pool_send, pool_recv, weight_sem, limited_sem, mean_sem, half_send, half_recv, *rest = rest
    later = [None] + [rest[9 * s : 9 * s + 9] for s in range(stages - 1)]
    targets, slots, nodes, _ = weights.shape
    levels = sources.shape[1]
    pieces = pl.cdiv(levels, WIDTH)
    groups = targets // GROUP
    share = nodes // n_mem
    me = lax.axis_index("cpl")
    member = lax.axis_index("mem")
    bits = [lax.rem(lax.div(member, 1 << s), 2) for s in range(stages)]
    partners = [member + (1 - 2 * bits[s]) * (1 << s) for s in range(stages)]

    weight_copy = pltpu.make_async_copy(weights, held, weight_sem)
    weight_copy.start()

    barrier = pltpu.get_barrier_semaphore()

    @pl.loop(1, n_cpl)
    def _(distance):
        pl.semaphore_signal(
            barrier, inc=1, device_id={"cpl": lax.rem(me + distance, n_cpl)}, device_id_type=MESH
        )

    for s in range(stages):
        pl.semaphore_signal(barrier, inc=1, device_id={"mem": partners[s]}, device_id_type=MESH)

    def rows_of(piece):
        return piece * WIDTH, min(WIDTH, levels - piece * WIDTH)

    def pool_copy(piece, distance, slot):
        start, size = rows_of(piece)
        return pltpu.make_async_remote_copy(
            src_ref=outgoing.at[distance - 1, pl.ds(start, size)],
            dst_ref=pool.at[slot, pl.ds(start, size)],
            send_sem=pool_send.at[piece, distance - 1],
            recv_sem=pool_recv.at[piece, distance - 1],
            device_id={"cpl": lax.rem(me + distance, n_cpl)},
            device_id_type=MESH,
        )

    def fill(piece):
        start, size = rows_of(piece)

        @pl.loop(1, n_cpl)
        def _(distance):
            chosen = send_pick[me, lax.rem(me + distance, n_cpl)]
            outgoing[distance - 1, pl.ds(start, size)] = sources[chosen, pl.ds(start, size)]

    def send(piece):
        @pl.loop(1, n_cpl)
        def _(distance):
            pool_copy(piece, distance, me).start()

    fill(0)
    pl.semaphore_wait(barrier, n_cpl - 1 + stages)
    send(0)
    for piece in range(1, pieces):
        fill(piece)
        if piece < AHEAD:
            send(piece)

    own = send_pick[me, me]
    pool[me, pl.ds(0, levels)] = sources[own]
    if pieces * WIDTH > levels:
        tail = pieces * WIDTH - levels
        pool[:, pl.ds(levels, tail)] = jnp.zeros((n_cpl, tail, nodes), pool.dtype)
    flipped[n_cpl] = jnp.zeros(flipped.shape[1:], flipped.dtype)
    weight_copy.wait()

    def half_copy(piece, group):
        return pltpu.make_async_remote_copy(
            src_ref=halves.at[piece, group, 1 - bits[0]],
            dst_ref=first_landed.at[piece, group],
            send_sem=half_send.at[piece, group],
            recv_sem=half_recv.at[piece, group],
            device_id={"mem": partners[0]},
            device_id_type=MESH,
        )

    def later_copies(s, piece, group):
        _, codes, codes_in, peaks, peaks_in, *sems = later[s]
        return [
            pltpu.make_async_remote_copy(
                src_ref=source.at[piece, group],
                dst_ref=target.at[piece, group],
                send_sem=send_sem.at[piece, group],
                recv_sem=recv_sem.at[piece, group],
                device_id={"mem": partners[s]},
                device_id_type=MESH,
            )
            for source, target, send_sem, recv_sem in (
                (codes, codes_in, sems[0], sems[1]),
                (peaks, peaks_in, sems[2], sems[3]),
            )
        ]

    def combined(s, piece, group, q):
        if s == 1:
            return halves[piece, group, bits[0], q] + first_landed[piece, group, q]
        kept, _, codes_in, _, peaks_in, *_ = later[s - 1]
        arrived = codes_in[piece, group, q].astype(jnp.int32).astype(jnp.float32)
        scale = peaks_in[piece, group] * (1.0 / STEPS)
        return kept[piece, group, q] + arrived * scale[:, None, :]

    def remap(piece, target):
        start, size = rows_of(piece)
        count = cover_count[target]
        first = cover_source[target, 0]
        terms, lowest, highest = [], [], []
        for k in range(slots):
            block = cover_source[target, k]
            live = k < count
            terms.append(flipped[jnp.where(live, block, n_cpl)])
            ranged = jnp.where(live, block, first)
            lowest.append(low[ranged])
            highest.append(high[ranged])
        left = jnp.concatenate([held[target, k] for k in range(slots)], axis=1)
        right = jnp.concatenate(terms, axis=0)
        summed = jnp.dot(left, right, preferred_element_type=jnp.float32)
        lower = functools.reduce(jnp.minimum, lowest)
        upper = functools.reduce(jnp.maximum, highest)
        center = jnp.sum(summed, axis=0, keepdims=True) * (1.0 / nodes)
        top = jnp.max(summed, axis=0, keepdims=True)
        bottom = jnp.min(summed, axis=0, keepdims=True)
        rising = (upper - center) / (top - center + 0.25)
        falling = (center - lower) / (center - bottom + 0.25)
        factor = jnp.clip(jnp.minimum(rising, falling), 0.0, 1.0)
        limited = center + factor * (summed - center)
        turned = limited.astype(jnp.bfloat16).T
        limited_out[target, pl.ds(start, size)] = turned[:size]
        return limited

    def limited_copy(piece):
        start, size = rows_of(piece)
        return pltpu.make_async_copy(
            limited_out.at[:, pl.ds(start, size)],
            remapped.at[:, pl.ds(start, size)],
            limited_sem.at[piece],
        )

    def mean_copy(piece):
        start, size = rows_of(piece)
        return pltpu.make_async_copy(
            mean_out.at[:, :, pl.ds(start, size)],
            ens_mean.at[:, :, pl.ds(start, size)],
            mean_sem.at[piece],
        )

    def collect(piece):
        start, size = rows_of(piece)
        for group in range(groups):
            if stages > 1:
                for copy in later_copies(stages - 1, piece, group):
                    copy.wait_recv()
            total = combined(stages, piece, group, 0)
            mean_out[pl.ds(group * GROUP, GROUP), :, pl.ds(start, size)] = (
                total * (1.0 / n_mem)
            )[:, :, :size]
        mean_copy(piece).start()

    for piece in range(pieces):
        start, size = rows_of(piece)

        @pl.loop(1, n_cpl)
        def _(distance):
            pool_copy(piece, distance, lax.rem(me - distance + n_cpl, n_cpl)).wait_recv()

        if piece + AHEAD < pieces:
            send(piece + AHEAD)

        @pl.loop(0, n_cpl)
        def _(block):
            values = pool[block, pl.ds(piece * WIDTH, WIDTH)].T
            flipped[block] = values
            wide = values.astype(jnp.float32)
            low[block] = jnp.min(wide, axis=0, keepdims=True)
            high[block] = jnp.max(wide, axis=0, keepdims=True)

        @pl.loop(0, groups)
        def _(group):
            for one in range(GROUP):
                limited = remap(piece, group * GROUP + one)
                for q in range(n_mem):
                    halves[piece, group, q % 2, q // 2, one] = limited[q * share : (q + 1) * share]
            half_copy(piece, group).start()

        limited_copy(piece).start()
        for s in range(1, stages):
            for group in range(groups):
                if s == 1:
                    half_copy(piece, group).wait_recv()
                else:
                    for copy in later_copies(s - 1, piece, group):
                        copy.wait_recv()
                kept, codes, _, peaks, *_ = later[s]
                parts = range((n_mem >> s) // 2)
                going = [combined(s, piece, group, 2 * q + 1 - bits[s]) for q in parts]
                peak = functools.reduce(
                    jnp.maximum, [jnp.max(jnp.abs(one), axis=1) for one in going]
                )
                peak = jnp.maximum(peak, 1e-30)
                peaks[piece, group] = peak
                factor = (STEPS / peak)[:, None, :]
                for q in parts:
                    codes[piece, group, q] = (
                        jnp.round(going[q] * factor).astype(jnp.int32).astype(jnp.int16)
                    )
                for copy in later_copies(s, piece, group):
                    copy.start()
                for q in parts:
                    kept[piece, group, q] = combined(s, piece, group, 2 * q + bits[s])
        if piece > 0:
            collect(piece - 1)
    collect(pieces - 1)

    for piece in range(pieces):

        @pl.loop(1, n_cpl)
        def _(distance):
            pool_copy(piece, distance, me).wait_send()

        for group in range(groups):
            half_copy(piece, group).wait_send()
            for s in range(1, stages):
                for copy in later_copies(s, piece, group):
                    copy.wait_send()
        limited_copy(piece).wait()
        mean_copy(piece).wait()


def local(n_cpl, n_mem, sources, weights, cover_source, cover_count, send_pick):
    blocks, nodes, members, levels = sources.shape
    targets, slots = cover_source.shape
    pieces = pl.cdiv(levels, WIDTH)
    padded = pieces * WIDTH
    groups = targets // GROUP
    share = nodes // n_mem
    stages = n_mem.bit_length() - 1
    turned = jnp.transpose(sources, (0, 2, 3, 1)).reshape(blocks, levels, nodes)
    lead = (pieces, groups)
    pairs = pltpu.SemaphoreType.DMA(lead)
    half = lead + (n_mem // 2, GROUP, share, WIDTH)
    halves = pltpu.VMEM(lead + (2, n_mem // 2, GROUP, share, WIDTH), jnp.float32)
    later = []
    for s in range(1, stages):
        part = lead + ((n_mem >> s) // 2, GROUP, share, WIDTH)
        peak = pltpu.VMEM(lead + (GROUP, WIDTH), jnp.float32)
        later += [
            pltpu.VMEM(part, jnp.float32),
            pltpu.VMEM(part, jnp.int16),
            pltpu.VMEM(part, jnp.int16),
            peak,
            peak,
            *[pairs] * 4,
        ]
    vmem = pl.BlockSpec(memory_space=pltpu.VMEM)
    whole = pl.BlockSpec(memory_space=pl.ANY)
    smem = pl.BlockSpec(memory_space=pltpu.SMEM)
    remapped, ens_mean = pl.pallas_call(
        functools.partial(kernel, n_cpl, n_mem),
        out_shape=(
            pltpu.VMEM((targets, levels, nodes), jnp.bfloat16),
            pltpu.VMEM((targets, share, levels), jnp.float32),
        ),
        in_specs=[smem, smem, smem, vmem, whole],
        out_specs=(whole, whole),
        scratch_shapes=[
            pltpu.VMEM((n_cpl - 1, levels, nodes), jnp.bfloat16),
            pltpu.VMEM((n_cpl, padded, nodes), jnp.bfloat16),
            pltpu.VMEM((n_cpl + 1, nodes, WIDTH), jnp.bfloat16),
            pltpu.VMEM((n_cpl, 1, WIDTH), jnp.float32),
            pltpu.VMEM((n_cpl, 1, WIDTH), jnp.float32),
            pltpu.VMEM((targets, slots, nodes, nodes), jnp.bfloat16),
            pltpu.VMEM((targets, levels, nodes), jnp.bfloat16),
            pltpu.VMEM((targets, share, levels), jnp.float32),
            halves,
            pltpu.VMEM(half, jnp.float32),
            pltpu.SemaphoreType.DMA((pieces, n_cpl - 1)),
            pltpu.SemaphoreType.DMA((pieces, n_cpl - 1)),
            pltpu.SemaphoreType.DMA,
            pltpu.SemaphoreType.DMA((pieces,)),
            pltpu.SemaphoreType.DMA((pieces,)),
            pairs,
            pairs,
            *later,
        ],
        compiler_params=pltpu.CompilerParams(
            collective_id=0, has_side_effects=True, vmem_limit_bytes=56 * 1024 * 1024
        ),
        cost_estimate=pl.CostEstimate(
            flops=2 * targets * slots * nodes * nodes * levels,
            bytes_accessed=weights.size * 2 + targets * levels * nodes * 4,
            transcendentals=0,
        ),
    )(cover_source, cover_count, send_pick, turned, weights)
    remapped = jnp.transpose(remapped.reshape(targets, members, levels, nodes), (0, 3, 1, 2))
    return remapped, ens_mean


def solution(mesh):
    placed = (
        P(("grp", "cpl"), None, "mem", None),
        P(("grp", "cpl"), None, None, None),
        P(("grp", "cpl"), None),
        P(("grp", "cpl")),
        P("grp", None),
    )
    return jax.shard_map(
        functools.partial(local, mesh.shape["cpl"], mesh.shape["mem"]),
        mesh=mesh,
        in_specs=placed,
        out_specs=(P(("grp", "cpl"), None, "mem", None), P(("grp", "cpl"), "mem", None)),
        check_vma=False,
    )
```

```python
import functools

import jax
import jax.numpy as jnp
from jax import lax
from jax.experimental import pallas as pl
from jax.experimental.pallas import tpu as pltpu
from jax.sharding import PartitionSpec as P

MESH = pl.DeviceIdType.MESH
WIDTH = 128
AHEAD = 2
STEPS = 32000.0
GROUP = 4


def kernel(
    n_cpl,
    n_mem,
    cover_source,
    cover_count,
    send_pick,
    sources,
    weights,
    remapped,
    ens_mean,
    outgoing,
    pool,
    flipped,
    low,
    high,
    held,
    *rest,
):
    stages = n_mem.bit_length() - 1
    halves, first_landed, *rest = rest
    pool_send, pool_recv, weight_sem, half_send, half_recv, *rest = rest
    later = [None] + [rest[9 * s : 9 * s + 9] for s in range(stages - 1)]
    targets, slots, nodes, _ = weights.shape
    levels = sources.shape[1]
    pieces = pl.cdiv(levels, WIDTH)
    groups = targets // GROUP
    share = nodes // n_mem
    me = lax.axis_index("cpl")
    member = lax.axis_index("mem")
    bits = [lax.rem(lax.div(member, 1 << s), 2) for s in range(stages)]
    partners = [member + (1 - 2 * bits[s]) * (1 << s) for s in range(stages)]

    weight_copy = pltpu.make_async_copy(weights, held, weight_sem)
    weight_copy.start()

    barrier = pltpu.get_barrier_semaphore()

    @pl.loop(1, n_cpl)
    def _(distance):
        pl.semaphore_signal(
            barrier, inc=1, device_id={"cpl": lax.rem(me + distance, n_cpl)}, device_id_type=MESH
        )

    for s in range(stages):
        pl.semaphore_signal(barrier, inc=1, device_id={"mem": partners[s]}, device_id_type=MESH)

    def rows_of(piece):
        return piece * WIDTH, min(WIDTH, levels - piece * WIDTH)

    def pool_copy(piece, distance, slot):
        start, size = rows_of(piece)
        return pltpu.make_async_remote_copy(
            src_ref=outgoing.at[distance - 1, pl.ds(start, size)],
            dst_ref=pool.at[slot, pl.ds(start, size)],
            send_sem=pool_send.at[piece, distance - 1],
            recv_sem=pool_recv.at[piece, distance - 1],
            device_id={"cpl": lax.rem(me + distance, n_cpl)},
            device_id_type=MESH,
        )

    def fill(piece):
        start, size = rows_of(piece)

        @pl.loop(1, n_cpl)
        def _(distance):
            chosen = send_pick[me, lax.rem(me + distance, n_cpl)]
            outgoing[distance - 1, pl.ds(start, size)] = sources[chosen, pl.ds(start, size)]

    def send(piece):
        @pl.loop(1, n_cpl)
        def _(distance):
            pool_copy(piece, distance, me).start()

    fill(0)
    pl.semaphore_wait(barrier, n_cpl - 1 + stages)
    send(0)
    for piece in range(1, pieces):
        fill(piece)
        if piece < AHEAD:
            send(piece)

    own = send_pick[me, me]
    pool[me, pl.ds(0, levels)] = sources[own]
    if pieces * WIDTH > levels:
        tail = pieces * WIDTH - levels
        pool[:, pl.ds(levels, tail)] = jnp.zeros((n_cpl, tail, nodes), pool.dtype)
    flipped[n_cpl] = jnp.zeros(flipped.shape[1:], flipped.dtype)
    weight_copy.wait()

    def half_copy(piece, group):
        return pltpu.make_async_remote_copy(
            src_ref=halves.at[piece, group, 1 - bits[0]],
            dst_ref=first_landed.at[piece, group],
            send_sem=half_send.at[piece, group],
            recv_sem=half_recv.at[piece, group],
            device_id={"mem": partners[0]},
            device_id_type=MESH,
        )

    def later_copies(s, piece, group):
        _, codes, codes_in, peaks, peaks_in, *sems = later[s]
        return [
            pltpu.make_async_remote_copy(
                src_ref=source.at[piece, group],
                dst_ref=target.at[piece, group],
                send_sem=send_sem.at[piece, group],
                recv_sem=recv_sem.at[piece, group],
                device_id={"mem": partners[s]},
                device_id_type=MESH,
            )
            for source, target, send_sem, recv_sem in (
                (codes, codes_in, sems[0], sems[1]),
                (peaks, peaks_in, sems[2], sems[3]),
            )
        ]

    def combined(s, piece, group, q):
        if s == 1:
            return halves[piece, group, bits[0], q] + first_landed[piece, group, q]
        kept, _, codes_in, _, peaks_in, *_ = later[s - 1]
        arrived = codes_in[piece, group, q].astype(jnp.int32).astype(jnp.float32)
        scale = peaks_in[piece, group] * (1.0 / STEPS)
        return kept[piece, group, q] + arrived * scale[:, None, :]

    def remap(piece, target):
        start, size = rows_of(piece)
        count = cover_count[target]
        first = cover_source[target, 0]
        terms, lowest, highest = [], [], []
        for k in range(slots):
            block = cover_source[target, k]
            live = k < count
            terms.append(flipped[jnp.where(live, block, n_cpl)])
            ranged = jnp.where(live, block, first)
            lowest.append(low[ranged])
            highest.append(high[ranged])
        left = jnp.concatenate([held[target, k] for k in range(slots)], axis=1)
        right = jnp.concatenate(terms, axis=0)
        summed = jnp.dot(left, right, preferred_element_type=jnp.float32)
        lower = functools.reduce(jnp.minimum, lowest)
        upper = functools.reduce(jnp.maximum, highest)
        center = jnp.sum(summed, axis=0, keepdims=True) * (1.0 / nodes)
        top = jnp.max(summed, axis=0, keepdims=True)
        bottom = jnp.min(summed, axis=0, keepdims=True)
        rising = (upper - center) / (top - center + 0.25)
        falling = (center - lower) / (center - bottom + 0.25)
        factor = jnp.clip(jnp.minimum(rising, falling), 0.0, 1.0)
        limited = center + factor * (summed - center)
        turned = limited.astype(jnp.bfloat16).T
        remapped[target, pl.ds(start, size)] = turned[:size]
        return limited

    def collect(piece):
        start, size = rows_of(piece)
        for group in range(groups):
            if stages > 1:
                for copy in later_copies(stages - 1, piece, group):
                    copy.wait_recv()
            total = combined(stages, piece, group, 0)
            ens_mean[pl.ds(group * GROUP, GROUP), :, pl.ds(start, size)] = (
                total * (1.0 / n_mem)
            )[:, :, :size]

    for piece in range(pieces):
        start, size = rows_of(piece)

        @pl.loop(1, n_cpl)
        def _(distance):
            pool_copy(piece, distance, lax.rem(me - distance + n_cpl, n_cpl)).wait_recv()

        if piece + AHEAD < pieces:
            send(piece + AHEAD)

        @pl.loop(0, n_cpl, unroll=n_cpl <= 4)
        def _(block):
            values = pool[block, pl.ds(piece * WIDTH, WIDTH)].T
            flipped[block] = values
            wide = values.astype(jnp.float32)
            low[block] = jnp.min(wide, axis=0, keepdims=True)
            high[block] = jnp.max(wide, axis=0, keepdims=True)

        for group in range(groups):
            for one in range(GROUP):
                limited = remap(piece, group * GROUP + one)
                for q in range(n_mem):
                    halves[piece, group, q % 2, q // 2, one] = limited[q * share : (q + 1) * share]
            half_copy(piece, group).start()

        for s in range(1, stages):
            for group in range(groups):
                if s == 1:
                    half_copy(piece, group).wait_recv()
                else:
                    for copy in later_copies(s - 1, piece, group):
                        copy.wait_recv()
                kept, codes, _, peaks, *_ = later[s]
                parts = range((n_mem >> s) // 2)
                going = [combined(s, piece, group, 2 * q + 1 - bits[s]) for q in parts]
                peak = functools.reduce(
                    jnp.maximum, [jnp.max(jnp.abs(one), axis=1) for one in going]
                )
                peak = jnp.maximum(peak, 1e-30)
                peaks[piece, group] = peak
                factor = (STEPS / peak)[:, None, :]
                for q in parts:
                    codes[piece, group, q] = (
                        jnp.round(going[q] * factor).astype(jnp.int32).astype(jnp.int16)
                    )
                for copy in later_copies(s, piece, group):
                    copy.start()
                for q in parts:
                    kept[piece, group, q] = combined(s, piece, group, 2 * q + bits[s])
        if piece > 0:
            collect(piece - 1)
    collect(pieces - 1)

    for piece in range(pieces):

        @pl.loop(1, n_cpl)
        def _(distance):
            pool_copy(piece, distance, me).wait_send()

        for group in range(groups):
            half_copy(piece, group).wait_send()
            for s in range(1, stages):
                for copy in later_copies(s, piece, group):
                    copy.wait_send()


def local(n_cpl, n_mem, sources, weights, cover_source, cover_count, send_pick):
    blocks, nodes, members, levels = sources.shape
    targets, slots = cover_source.shape
    pieces = pl.cdiv(levels, WIDTH)
    padded = pieces * WIDTH
    groups = targets // GROUP
    share = nodes // n_mem
    stages = n_mem.bit_length() - 1
    turned = jnp.transpose(sources, (0, 2, 3, 1)).reshape(blocks, levels, nodes)
    lead = (pieces, groups)
    pairs = pltpu.SemaphoreType.DMA(lead)
    half = lead + (n_mem // 2, GROUP, share, WIDTH)
    halves = pltpu.VMEM(lead + (2, n_mem // 2, GROUP, share, WIDTH), jnp.float32)
    later = []
    for s in range(1, stages):
        part = lead + ((n_mem >> s) // 2, GROUP, share, WIDTH)
        peak = pltpu.VMEM(lead + (GROUP, WIDTH), jnp.float32)
        later += [
            pltpu.VMEM(part, jnp.float32),
            pltpu.VMEM(part, jnp.int16),
            pltpu.VMEM(part, jnp.int16),
            peak,
            peak,
            *[pairs] * 4,
        ]
    vmem = pl.BlockSpec(memory_space=pltpu.VMEM)
    whole = pl.BlockSpec(memory_space=pl.ANY)
    smem = pl.BlockSpec(memory_space=pltpu.SMEM)
    remapped, ens_mean = pl.pallas_call(
        functools.partial(kernel, n_cpl, n_mem),
        out_shape=(
            pltpu.VMEM((targets, levels, nodes), jnp.bfloat16),
            pltpu.VMEM((targets, share, levels), jnp.float32),
        ),
        in_specs=[smem, smem, smem, vmem, whole],
        out_specs=(vmem, vmem),
        scratch_shapes=[
            pltpu.VMEM((n_cpl - 1, levels, nodes), jnp.bfloat16),
            pltpu.VMEM((n_cpl, padded, nodes), jnp.bfloat16),
            pltpu.VMEM((n_cpl + 1, nodes, WIDTH), jnp.bfloat16),
            pltpu.VMEM((n_cpl, 1, WIDTH), jnp.float32),
            pltpu.VMEM((n_cpl, 1, WIDTH), jnp.float32),
            pltpu.VMEM((targets, slots, nodes, nodes), jnp.bfloat16),
            halves,
            pltpu.VMEM(half, jnp.float32),
            pltpu.SemaphoreType.DMA((pieces, n_cpl - 1)),
            pltpu.SemaphoreType.DMA((pieces, n_cpl - 1)),
            pltpu.SemaphoreType.DMA,
            pairs,
            pairs,
            *later,
        ],
        compiler_params=pltpu.CompilerParams(
            collective_id=0, has_side_effects=True, vmem_limit_bytes=56 * 1024 * 1024
        ),
        cost_estimate=pl.CostEstimate(
            flops=2 * targets * slots * nodes * nodes * levels,
            bytes_accessed=weights.size * 2 + targets * levels * nodes * 4,
            transcendentals=0,
        ),
    )(cover_source, cover_count, send_pick, turned, weights)
    remapped = jnp.transpose(remapped.reshape(targets, members, levels, nodes), (0, 3, 1, 2))
    return remapped, ens_mean


def solution(mesh):
    placed = (
        P(("grp", "cpl"), None, "mem", None),
        P(("grp", "cpl"), None, None, None),
        P(("grp", "cpl"), None),
        P(("grp", "cpl")),
        P("grp", None),
    )
    return jax.shard_map(
        functools.partial(local, mesh.shape["cpl"], mesh.shape["mem"]),
        mesh=mesh,
        in_specs=placed,
        out_specs=(P(("grp", "cpl"), None, "mem", None), P(("grp", "cpl"), "mem", None)),
        check_vma=False,
    )
```

```python
import functools

import jax
import jax.numpy as jnp
from jax import lax
from jax.experimental import pallas as pl
from jax.experimental.pallas import tpu as pltpu
from jax.sharding import PartitionSpec as P

MESH = pl.DeviceIdType.MESH
WIDTH = 128
AHEAD = 2
STEPS = 32000.0
GROUP = 4


def kernel(
    n_cpl,
    n_mem,
    cover_source,
    cover_count,
    send_pick,
    sources,
    weights,
    remapped,
    ens_mean,
    outgoing,
    pool,
    flipped,
    low,
    high,
    held,
    *rest,
):
    stages = n_mem.bit_length() - 1
    halves, first_landed, *rest = rest
    pool_send, pool_recv, weight_sem, half_send, half_recv, *rest = rest
    later = [None] + [rest[9 * s : 9 * s + 9] for s in range(stages - 1)]
    targets, slots, nodes, _ = weights.shape
    levels = sources.shape[1]
    pieces = pl.cdiv(levels, WIDTH)
    groups = targets // GROUP
    share = nodes // n_mem
    me = lax.axis_index("cpl")
    member = lax.axis_index("mem")
    bits = [lax.rem(lax.div(member, 1 << s), 2) for s in range(stages)]
    partners = [member + (1 - 2 * bits[s]) * (1 << s) for s in range(stages)]

    weight_copy = pltpu.make_async_copy(weights, held, weight_sem)
    weight_copy.start()

    barrier = pltpu.get_barrier_semaphore()

    @pl.loop(1, n_cpl)
    def _(distance):
        pl.semaphore_signal(
            barrier, inc=1, device_id={"cpl": lax.rem(me + distance, n_cpl)}, device_id_type=MESH
        )

    for s in range(stages):
        pl.semaphore_signal(barrier, inc=1, device_id={"mem": partners[s]}, device_id_type=MESH)

    def rows_of(piece):
        return piece * WIDTH, min(WIDTH, levels - piece * WIDTH)

    def pool_copy(piece, distance, slot):
        start, size = rows_of(piece)
        return pltpu.make_async_remote_copy(
            src_ref=outgoing.at[distance - 1, pl.ds(start, size)],
            dst_ref=pool.at[slot, pl.ds(start, size)],
            send_sem=pool_send.at[piece, distance - 1],
            recv_sem=pool_recv.at[piece, distance - 1],
            device_id={"cpl": lax.rem(me + distance, n_cpl)},
            device_id_type=MESH,
        )

    def fill(piece):
        start, size = rows_of(piece)

        @pl.loop(1, n_cpl)
        def _(distance):
            chosen = send_pick[me, lax.rem(me + distance, n_cpl)]
            outgoing[distance - 1, pl.ds(start, size)] = sources[chosen, pl.ds(start, size)]

    def send(piece):
        @pl.loop(1, n_cpl)
        def _(distance):
            pool_copy(piece, 1 + lax.rem(distance + n_cpl // 2 - 2, n_cpl - 1), me).start()

    fill(0)
    pl.semaphore_wait(barrier, n_cpl - 1 + stages)
    send(0)
    for piece in range(1, pieces):
        fill(piece)
        if piece < AHEAD:
            send(piece)

    own = send_pick[me, me]
    pool[me, pl.ds(0, levels)] = sources[own]
    if pieces * WIDTH > levels:
        tail = pieces * WIDTH - levels
        pool[:, pl.ds(levels, tail)] = jnp.zeros((n_cpl, tail, nodes), pool.dtype)
    flipped[n_cpl] = jnp.zeros(flipped.shape[1:], flipped.dtype)
    weight_copy.wait()

    def half_copy(piece, group):
        return pltpu.make_async_remote_copy(
            src_ref=halves.at[piece, group, 1 - bits[0]],
            dst_ref=first_landed.at[piece, group],
            send_sem=half_send.at[piece, group],
            recv_sem=half_recv.at[piece, group],
            device_id={"mem": partners[0]},
            device_id_type=MESH,
        )

    def later_copies(s, piece, group):
        _, codes, codes_in, peaks, peaks_in, *sems = later[s]
        return [
            pltpu.make_async_remote_copy(
                src_ref=source.at[piece, group],
                dst_ref=target.at[piece, group],
                send_sem=send_sem.at[piece, group],
                recv_sem=recv_sem.at[piece, group],
                device_id={"mem": partners[s]},
                device_id_type=MESH,
            )
            for source, target, send_sem, recv_sem in (
                (codes, codes_in, sems[0], sems[1]),
                (peaks, peaks_in, sems[2], sems[3]),
            )
        ]

    def combined(s, piece, group, q):
        if s == 1:
            return halves[piece, group, bits[0], q] + first_landed[piece, group, q]
        kept, _, codes_in, _, peaks_in, *_ = later[s - 1]
        arrived = codes_in[piece, group, q].astype(jnp.int32).astype(jnp.float32)
        scale = peaks_in[piece, group] * (1.0 / STEPS)
        return kept[piece, group, q] + arrived * scale[:, None, :]

    def remap(piece, target):
        start, size = rows_of(piece)
        count = cover_count[target]
        first = cover_source[target, 0]
        terms, lowest, highest = [], [], []
        for k in range(slots):
            block = cover_source[target, k]
            live = k < count
            terms.append(flipped[jnp.where(live, block, n_cpl)])
            ranged = jnp.where(live, block, first)
            lowest.append(low[ranged])
            highest.append(high[ranged])
        left = jnp.concatenate([held[target, k] for k in range(slots)], axis=1)
        right = jnp.concatenate(terms, axis=0)
        summed = jnp.dot(left, right, preferred_element_type=jnp.float32)
        lower = functools.reduce(jnp.minimum, lowest)
        upper = functools.reduce(jnp.maximum, highest)
        center = jnp.sum(summed, axis=0, keepdims=True) * (1.0 / nodes)
        top = jnp.max(summed, axis=0, keepdims=True)
        bottom = jnp.min(summed, axis=0, keepdims=True)
        rising = (upper - center) / (top - center + 0.25)
        falling = (center - lower) / (center - bottom + 0.25)
        factor = jnp.clip(jnp.minimum(rising, falling), 0.0, 1.0)
        limited = center + factor * (summed - center)
        turned = limited.astype(jnp.bfloat16).T
        remapped[target, pl.ds(start, size)] = turned[:size]
        return limited

    def collect(piece):
        start, size = rows_of(piece)
        for group in range(groups):
            if stages > 1:
                for copy in later_copies(stages - 1, piece, group):
                    copy.wait_recv()
            total = combined(stages, piece, group, 0)
            ens_mean[pl.ds(group * GROUP, GROUP), :, pl.ds(start, size)] = (
                total * (1.0 / n_mem)
            )[:, :, :size]

    for piece in range(pieces):
        start, size = rows_of(piece)

        @pl.loop(1, n_cpl)
        def _(distance):
            pool_copy(piece, distance, lax.rem(me - distance + n_cpl, n_cpl)).wait_recv()

        if piece + AHEAD < pieces:
            send(piece + AHEAD)

        @pl.loop(0, n_cpl, unroll=n_cpl <= 4)
        def _(block):
            values = pool[block, pl.ds(piece * WIDTH, WIDTH)].T
            flipped[block] = values
            wide = values.astype(jnp.float32)
            low[block] = jnp.min(wide, axis=0, keepdims=True)
            high[block] = jnp.max(wide, axis=0, keepdims=True)

        for group in range(groups):
            for one in range(GROUP):
                limited = remap(piece, group * GROUP + one)
                for q in range(n_mem):
                    halves[piece, group, q % 2, q // 2, one] = limited[q * share : (q + 1) * share]
            half_copy(piece, group).start()

        for s in range(1, stages):
            for group in range(groups):
                if s == 1:
                    half_copy(piece, group).wait_recv()
                else:
                    for copy in later_copies(s - 1, piece, group):
                        copy.wait_recv()
                kept, codes, _, peaks, *_ = later[s]
                parts = range((n_mem >> s) // 2)
                going = [combined(s, piece, group, 2 * q + 1 - bits[s]) for q in parts]
                peak = functools.reduce(
                    jnp.maximum, [jnp.max(jnp.abs(one), axis=1) for one in going]
                )
                peak = jnp.maximum(peak, 1e-30)
                peaks[piece, group] = peak
                factor = (STEPS / peak)[:, None, :]
                for q in parts:
                    codes[piece, group, q] = (
                        jnp.round(going[q] * factor).astype(jnp.int32).astype(jnp.int16)
                    )
                for copy in later_copies(s, piece, group):
                    copy.start()
                for q in parts:
                    kept[piece, group, q] = combined(s, piece, group, 2 * q + bits[s])
        if piece > 0:
            collect(piece - 1)
    collect(pieces - 1)

    for piece in range(pieces):

        @pl.loop(1, n_cpl)
        def _(distance):
            pool_copy(piece, distance, me).wait_send()

        for group in range(groups):
            half_copy(piece, group).wait_send()
            for s in range(1, stages):
                for copy in later_copies(s, piece, group):
                    copy.wait_send()


def local(n_cpl, n_mem, sources, weights, cover_source, cover_count, send_pick):
    blocks, nodes, members, levels = sources.shape
    targets, slots = cover_source.shape
    pieces = pl.cdiv(levels, WIDTH)
    padded = pieces * WIDTH
    groups = targets // GROUP
    share = nodes // n_mem
    stages = n_mem.bit_length() - 1
    turned = jnp.transpose(sources, (0, 2, 3, 1)).reshape(blocks, levels, nodes)
    lead = (pieces, groups)
    pairs = pltpu.SemaphoreType.DMA(lead)
    half = lead + (n_mem // 2, GROUP, share, WIDTH)
    halves = pltpu.VMEM(lead + (2, n_mem // 2, GROUP, share, WIDTH), jnp.float32)
    later = []
    for s in range(1, stages):
        part = lead + ((n_mem >> s) // 2, GROUP, share, WIDTH)
        peak = pltpu.VMEM(lead + (GROUP, WIDTH), jnp.float32)
        later += [
            pltpu.VMEM(part, jnp.float32),
            pltpu.VMEM(part, jnp.int16),
            pltpu.VMEM(part, jnp.int16),
            peak,
            peak,
            *[pairs] * 4,
        ]
    vmem = pl.BlockSpec(memory_space=pltpu.VMEM)
    whole = pl.BlockSpec(memory_space=pl.ANY)
    smem = pl.BlockSpec(memory_space=pltpu.SMEM)
    remapped, ens_mean = pl.pallas_call(
        functools.partial(kernel, n_cpl, n_mem),
        out_shape=(
            pltpu.VMEM((targets, levels, nodes), jnp.bfloat16),
            pltpu.VMEM((targets, share, levels), jnp.float32),
        ),
        in_specs=[smem, smem, smem, vmem, whole],
        out_specs=(vmem, vmem),
        scratch_shapes=[
            pltpu.VMEM((n_cpl - 1, levels, nodes), jnp.bfloat16),
            pltpu.VMEM((n_cpl, padded, nodes), jnp.bfloat16),
            pltpu.VMEM((n_cpl + 1, nodes, WIDTH), jnp.bfloat16),
            pltpu.VMEM((n_cpl, 1, WIDTH), jnp.float32),
            pltpu.VMEM((n_cpl, 1, WIDTH), jnp.float32),
            pltpu.VMEM((targets, slots, nodes, nodes), jnp.bfloat16),
            halves,
            pltpu.VMEM(half, jnp.float32),
            pltpu.SemaphoreType.DMA((pieces, n_cpl - 1)),
            pltpu.SemaphoreType.DMA((pieces, n_cpl - 1)),
            pltpu.SemaphoreType.DMA,
            pairs,
            pairs,
            *later,
        ],
        compiler_params=pltpu.CompilerParams(
            collective_id=0, has_side_effects=True, vmem_limit_bytes=56 * 1024 * 1024
        ),
        cost_estimate=pl.CostEstimate(
            flops=2 * targets * slots * nodes * nodes * levels,
            bytes_accessed=weights.size * 2 + targets * levels * nodes * 4,
            transcendentals=0,
        ),
    )(cover_source, cover_count, send_pick, turned, weights)
    remapped = jnp.transpose(remapped.reshape(targets, members, levels, nodes), (0, 3, 1, 2))
    return remapped, ens_mean


def solution(mesh):
    placed = (
        P(("grp", "cpl"), None, "mem", None),
        P(("grp", "cpl"), None, None, None),
        P(("grp", "cpl"), None),
        P(("grp", "cpl")),
        P("grp", None),
    )
    return jax.shard_map(
        functools.partial(local, mesh.shape["cpl"], mesh.shape["mem"]),
        mesh=mesh,
        in_specs=placed,
        out_specs=(P(("grp", "cpl"), None, "mem", None), P(("grp", "cpl"), "mem", None)),
        check_vma=False,
    )
```
